32 devices in a mesh: mem: 4 (over y, x), dom: 8 (over z, core).
Axes of the slice: x: 2, y: 2, z: 4, core: 2. Of those that a mesh axis runs over, the one named last changes fastest.
Arguments:
- state: bfloat16 [64, 6, 4, 256, 128], P('mem', None, None, 'dom'), may hold values from -6 to 6
- wind_x: float32 [4, 256, 128], P(None, 'dom'), may hold values from -0.5 to 0.5
- wind_y: float32 [4, 256, 128], P(None, 'dom'), may hold values from -0.5 to 0.5
- viscosity_numbers: float32 [6], replicated, may hold values from 0.02 to 0.2
- weights: float32 [256, 64, 64], P('dom'), may hold values from -0.75 to 0.75
- obs_count: int32 [256], replicated, may hold values from 0 to 45, as said below
- owner: int32 [256], replicated, may hold values from 0 to 7, as said below
Outputs:
- analysis: bfloat16 [64, 6, 4, 256, 128], P('mem', None, None, 'dom')
The draws below stay inside these ranges and needn't reach their ends.
Inputs may be any that keep to these rules, and one draw needn't show every extreme that they name: `obs_count`: block 0 has 45 observations. `owner`: each device's blocks, ranked by falling observation count (ties by position), are dealt to owners in turn, so that every device owns exactly 4 of each device's 32 blocks.
All inputs are finite; a program needn't handle non-finite values.
Results may differ from the reference program's by a relative error of at most 0.007.
Values may be sent and summed in bfloat16 or wider, within the bound.
A program may use at most 64 MiB of HBM per device.

```python
import math
import jax
import jax.numpy as jnp
from jax import lax

M = 64
F = 6
L = 4
CY = 32
NXC = 128
OBS_HALF = 8
NY = 256
CB = 4
N_DOM = 8


def block_counts(key):
    first, second = jax.random.split(key)
    level_draw = jax.random.randint(first, (NY // CY, 1), 0, 4)
    base_draw = jax.random.randint(second, (NY // CY, CY), 0, 16)
    counts = (level_draw * base_draw).reshape(NY)
    counts = counts.at[0].set(45)
    counts = counts.at[NY - 1].set(0)
    return counts.astype(jnp.int32)


def draw_obs_count(key, part):
    shared = block_counts(key)
    return shared


def draw_owner(key, part):
    shared = block_counts(key)
    sources = NY // CY
    counts = shared.reshape(sources, CY)
    position = jnp.arange(CY, dtype=jnp.int32)[None, :]
    scores = (60 - counts) * CY + position
    ordering = jnp.argsort(scores, axis=1, stable=True)
    ranking = jnp.argsort(ordering, axis=1, stable=True).astype(jnp.int32)
    source = jnp.arange(sources, dtype=jnp.int32)[:, None]
    return ((source + ranking) % sources).reshape(NY).astype(jnp.int32)


def shard_levels(stream_key, dims, shards, least, largest):
    factor_of, own = 1.0, jax.random.fold_in(stream_key, 6)
    for dim, shards_of in shards:
        steps = jnp.exp(jax.random.uniform(jax.random.fold_in(own, dim), (shards_of,), jnp.float32, least / len(shards), largest / len(shards)))
        factor_of = factor_of * jnp.repeat(steps, dims[dim] // shards_of).reshape([-1 if axis == dim else 1 for axis in range(len(dims))])
    return factor_of


def normal_values(stream_key, dims, deviation, limit, cuts=(), kind=jnp.bfloat16):
    factor_of = shard_levels(stream_key, dims, cuts, -0.22, 0.18) if cuts else 1.0
    values = jax.random.normal(stream_key, dims, jnp.float32) * deviation * factor_of
    return jnp.minimum(jnp.maximum(values, -limit), limit).astype(kind)


def setup_inputs(seed: int = 0) -> dict:
    key_of = jax.random.split(jax.random.key(seed), 8)
    state = normal_values(key_of[0], (M, F, L, NY, NXC), 1.0, 6.0, ((0, 4), (3, 8)))
    wind_x = jnp.clip(jax.random.uniform(key_of[1], (L, NY, NXC), jnp.float32, -0.5, 0.5) * shard_levels(key_of[1], (L, NY, NXC), ((1, 8),), -0.4, 0.0), -0.5, 0.5)
    wind_y = jnp.clip(jax.random.uniform(key_of[2], (L, NY, NXC), jnp.float32, -0.5, 0.5) * shard_levels(key_of[2], (L, NY, NXC), ((1, 8),), -0.4, 0.0), -0.5, 0.5)
    viscosity_numbers = jnp.clip(jnp.exp(jax.random.uniform(key_of[3], (F,), jnp.float32, math.log(0.02), math.log(0.2))), 0.02, 0.2)
    weights = normal_values(key_of[4], (NY, M, M), M ** -0.5, 0.75, ((0, 8),), jnp.float32)
    obs_count = draw_obs_count(jax.random.fold_in(key_of[7], 71), 0)
    owner = draw_owner(jax.random.fold_in(key_of[7], 71), 0)
    return dict(state=state, wind_x=wind_x, wind_y=wind_y, viscosity_numbers=viscosity_numbers, weights=weights, obs_count=obs_count, owner=owner)


def combined(weight, counts):
    number = counts.astype(jnp.float32)
    gain = number / (number + OBS_HALF)
    eye = jnp.eye(weight.shape[-1], dtype=jnp.float32)
    transform_weights_square = (1.0 - gain)[:, None, None] * eye + gain[:, None, None] * weight
    return (transform_weights_square - jnp.mean(transform_weights_square, axis=1, keepdims=True) + 1.0 / weight.shape[-1]).astype(jnp.bfloat16)


def predicted_height_index(height_section, zonal_velocity, meridional_velocity, viscosity_numbers):
    field = height_section.astype(jnp.float32)
    padded = jnp.pad(field, ((0, 0), (0, 0), (1, 1), (1, 1)))
    upper = padded[:, :, 2:, 1:-1]
    lower = padded[:, :, :-2, 1:-1]
    east = padded[:, :, 1:-1, 2:]
    west = padded[:, :, 1:-1, :-2]
    ensemble_spread = upper + lower + east + west - 4.0 * field
    carried_along = zonal_velocity * (east - west) + meridional_velocity * (upper - lower)
    return (field + viscosity_numbers[:, None, None] * ensemble_spread - 0.5 * carried_along).astype(jnp.bfloat16)


def reference(state, wind_x, wind_y, viscosity_numbers, weights, obs_count, owner):
    owner_all = owner.reshape(N_DOM, CY)
    onehot = (owner_all[:, :, None] == jnp.arange(N_DOM, dtype=jnp.int32)[None, None, :]).astype(jnp.int32)
    before = jnp.sum((jnp.cumsum(onehot, axis=1) - onehot) * onehot, axis=2)
    source = jnp.arange(N_DOM, dtype=jnp.int32)[:, None]
    slot = (owner_all * CY + source * CB + before).reshape(NY).astype(jnp.int32)
    transform_weights_square = combined(weights[slot], obs_count).astype(jnp.float32)

    def level(inputs):
        height_section, zonal_velocity, meridional_velocity = inputs
        predicted_prior = predicted_height_index(height_section, zonal_velocity, meridional_velocity, viscosity_numbers)
        transformed_posterior = jnp.einsum('pfrh,rps->sfrh', predicted_prior.astype(jnp.float32), transform_weights_square, precision=lax.Precision.HIGHEST)
        return transformed_posterior.astype(jnp.bfloat16)

    result = lax.map(level, (jnp.moveaxis(state, 2, 0), wind_x, wind_y))
    return jnp.moveaxis(result, 0, 2)
```

```python
import functools

import jax
import jax.numpy as jnp
from jax import lax
from jax.experimental import pallas as pl
from jax.experimental.pallas import tpu as pltpu
from jax.sharding import PartitionSpec as P

OBS_HALF = 8
GROUP = 16
STEP = 4
MESH = pl.DeviceIdType.MESH


def partner(me, count, step):
    if count == 4:
        return (me + 1 - 2 * (me % 2), (me + 2) % 4, 3 - me)[step - 1]
    return (me + step) % count


def sender(me, count, step):
    return partner(me, count, step) if count == 4 else (me + count - step) % count


def kernel(
    n_mem,
    n_dom,
    state,
    wind_x,
    wind_y,
    viscosity,
    weights,
    obs_count,
    owner,
    out,
    raw,
    low,
    high,
    fore,
    done,
    block_diag,
    stacked,
    weight_in,
    weight_out,
    home,
    wx,
    wy,
    sem_fwd_send,
    sem_fwd_recv,
    sem_own,
    sem_halo_send,
    sem_halo_recv,
    sem_ret_send,
    sem_ret_recv,
    sem_own_out,
    sem_w_send,
    sem_w_recv,
    sem_in,
):
    me = lax.axis_index("mem")
    here = lax.axis_index("dom")
    local, fields, _, rows, cells = state.shape
    members = local * n_mem
    per_owner = rows // n_dom
    groups = rows // GROUP

    weights_copy = pltpu.make_async_copy(weights, weight_in, sem_in.at[0])
    wx_copy = pltpu.make_async_copy(wind_x.at[me], wx, sem_in.at[1])
    wy_copy = pltpu.make_async_copy(wind_y.at[me], wy, sem_in.at[2])
    weights_copy.start()
    wx_copy.start()
    wy_copy.start()

    barrier = pltpu.get_barrier_semaphore()
    for step in range(1, n_mem):
        pl.semaphore_signal(
            barrier, inc=1, device_id=(partner(me, n_mem, step), here), device_id_type=MESH
        )

    def greet(step, carry):
        pl.semaphore_signal(
            barrier, inc=1, device_id=(me, (here + step) % n_dom), device_id_type=MESH
        )
        return carry

    lax.fori_loop(1, n_dom, greet, 0)
    pl.semaphore_wait(barrier, n_mem - 1 + n_dom - 1)

    def forward(step, field):
        to = partner(me, n_mem, step)
        return pltpu.make_async_remote_copy(
            src_ref=state.at[:, field, to],
            dst_ref=raw.at[field, pl.ds(me * local, local)],
            send_sem=sem_fwd_send.at[step - 1, field],
            recv_sem=sem_fwd_recv.at[step - 1, field],
            device_id=(to, here),
            device_id_type=MESH,
        )

    def own(field):
        return pltpu.make_async_copy(
            state.at[:, field, me], raw.at[field, pl.ds(me * local, local)], sem_own.at[field]
        )

    def halo_up(field):
        return pltpu.make_async_remote_copy(
            src_ref=raw.at[field, :, pl.ds(rows - GROUP, GROUP)],
            dst_ref=low.at[field],
            send_sem=sem_halo_send.at[0, field],
            recv_sem=sem_halo_recv.at[0, field],
            device_id=(me, (here + 1) % n_dom),
            device_id_type=MESH,
        )

    def halo_down(field):
        return pltpu.make_async_remote_copy(
            src_ref=raw.at[field, :, pl.ds(0, GROUP)],
            dst_ref=high.at[field],
            send_sem=sem_halo_send.at[1, field],
            recv_sem=sem_halo_recv.at[1, field],
            device_id=(me, (here + n_dom - 1) % n_dom),
            device_id_type=MESH,
        )

    def back(step, field):
        to = partner(me, n_mem, step)
        return pltpu.make_async_remote_copy(
            src_ref=done.at[field, pl.ds(to * local, local)],
            dst_ref=out.at[:, field, me],
            send_sem=sem_ret_send.at[step - 1, field],
            recv_sem=sem_ret_recv.at[step - 1, field],
            device_id=(to, here),
            device_id_type=MESH,
        )

    def own_out(field):
        return pltpu.make_async_copy(
            done.at[field, pl.ds(me * local, local)], out.at[:, field, me], sem_own_out.at[field]
        )

    def weight_to(step):
        to = (here + step) % n_dom
        return pltpu.make_async_remote_copy(
            src_ref=weight_out.at[pl.ds(to * per_owner, per_owner)],
            dst_ref=home.at[pl.ds(here * per_owner, per_owner)],
            send_sem=sem_w_send.at[step],
            recv_sem=sem_w_recv.at[step],
            device_id=(me, to),
            device_id_type=MESH,
        )

    def send_field(field, carry):
        for step in range(1, n_mem):
            forward(step, field).start()
        own(field).start()
        return carry

    lax.fori_loop(0, fields, send_field, 0)

    weights_copy.wait()

    def narrow(block, carry):
        weight_out[block] = weight_in[block].astype(jnp.bfloat16)
        return carry

    lax.fori_loop(0, rows, narrow, 0)

    def send_weight(step, carry):
        weight_to(step).start()
        return carry

    lax.fori_loop(1, n_dom, send_weight, 0)
    own_weight = pltpu.make_async_copy(
        weight_out.at[pl.ds(here * per_owner, per_owner)],
        home.at[pl.ds(here * per_owner, per_owner)],
        sem_in.at[3],
    )
    own_weight.start()

    @pl.when(here == 0)
    def _():
        low[...] = jnp.zeros_like(low)

    @pl.when(here == n_dom - 1)
    def _():
        high[...] = jnp.zeros_like(high)

    def share_edges(field):
        own(field).wait()
        for step in range(1, n_mem):
            forward(step, field).wait_recv()

        @pl.when(here < n_dom - 1)
        def _():
            halo_up(field).start()

        @pl.when(here > 0)
        def _():
            halo_down(field).start()

    own_weight.wait()

    def take_weight(step, carry):
        weight_to(step).wait_recv()
        return carry

    lax.fori_loop(1, n_dom, take_weight, 0)

    row_id = lax.broadcasted_iota(jnp.int32, (members, members), 0)
    col_id = lax.broadcasted_iota(jnp.int32, (members, members), 1)
    eye = (row_id == col_id).astype(jnp.float32)
    eye_narrow = eye.astype(jnp.bfloat16)
    base = here * rows

    def combine(block, carry):
        mine = owner[base + block]

        def count(other, total):
            return total + jnp.where(owner[base + other] == mine, 1, 0)

        rank = lax.fori_loop(0, block, count, 0)
        weight = home[mine * per_owner + rank].astype(jnp.float32)
        number = jnp.full((members, members), obs_count[base + block], jnp.int32).astype(
            jnp.float32
        )
        gain = number / (number + OBS_HALF)
        mixing = (1.0 - gain) * eye + gain * weight
        square = (
            mixing - jnp.mean(mixing, axis=0, keepdims=True) + 1.0 / members
        ).astype(jnp.bfloat16)
        flipped = lax.dot_general(
            square, eye_narrow, (((0,), (0,)), ((), ())), preferred_element_type=jnp.float32
        )
        group = block // GROUP
        place = block % GROUP
        stacked[group, pl.ds(place, members, stride=GROUP), pl.ds(0, members)] = flipped
        return carry

    lax.fori_loop(0, rows, combine, 0)

    wide = members * GROUP
    spread_row = lax.broadcasted_iota(jnp.int32, (members, wide), 0)
    spread_col = lax.broadcasted_iota(jnp.int32, (members, wide), 1)
    spread = ((spread_col >> 4) == spread_row).astype(jnp.bfloat16)
    piece = 64
    mask = (
        (lax.broadcasted_iota(jnp.int32, (piece, wide), 0) & (GROUP - 1))
        == (lax.broadcasted_iota(jnp.int32, (piece, wide), 1) & (GROUP - 1))
    )

    for group in range(groups):

        def widen(part, carry, group=group):
            start = pl.multiple_of(part * piece, piece)
            lines = stacked[group, pl.ds(start, piece), pl.ds(0, members)].astype(jnp.bfloat16)
            full = jnp.dot(lines, spread, preferred_element_type=jnp.float32)
            block_diag[group, pl.ds(start, piece)] = jnp.where(mask, full, 0.0).astype(
                jnp.bfloat16
            )
            return carry

        lax.fori_loop(0, wide // piece, widen, 0)

    wx_copy.wait()
    wy_copy.wait()
    share_edges(0)

    flat = STEP * rows
    line = lax.broadcasted_iota(jnp.int32, (flat, cells), 0) & (rows - 1)
    cell = lax.broadcasted_iota(jnp.int32, (flat, cells), 1)
    first_line, last_line = line == 0, line == rows - 1
    first_cell, last_cell = cell == 0, cell == cells - 1
    blank = jnp.zeros((STEP, rows - GROUP, cells), jnp.float32)

    def work(field, carry):
        @pl.when(field < fields - 1)
        def _():
            share_edges(field + 1)

        @pl.when(here > 0)
        def _():
            halo_up(field).wait_recv()

        @pl.when(here < n_dom - 1)
        def _():
            halo_down(field).wait_recv()

        number = viscosity[field]
        along = jnp.broadcast_to(wx[...][None], (STEP, rows, cells)).reshape(flat, cells)
        across = jnp.broadcast_to(wy[...][None], (STEP, rows, cells)).reshape(flat, cells)

        def stencil(part, inner):
            which = pl.ds(part * STEP, STEP)
            middle = raw[field, which].astype(jnp.float32).reshape(flat, cells)
            under = low[field, which].astype(jnp.float32).reshape(STEP * GROUP, cells)
            over = high[field, which].astype(jnp.float32).reshape(STEP * GROUP, cells)
            under = pltpu.roll(under, STEP * GROUP - (GROUP - 1), 0).reshape(STEP, GROUP, cells)
            over = pltpu.roll(over, GROUP - 1, 0).reshape(STEP, GROUP, cells)
            under = jnp.concatenate([under, blank], axis=1).reshape(flat, cells)
            over = jnp.concatenate([blank, over], axis=1).reshape(flat, cells)
            lower = jnp.where(first_line, under, pltpu.roll(middle, 1, 0))
            upper = jnp.where(last_line, over, pltpu.roll(middle, flat - 1, 0))
            west = jnp.where(first_cell, 0.0, pltpu.roll(middle, 1, 1))
            east = jnp.where(last_cell, 0.0, pltpu.roll(middle, cells - 1, 1))
            ensemble = upper + lower + east + west - 4.0 * middle
            carried = along * (east - west) + across * (upper - lower)
            prior = middle + number * ensemble - 0.5 * carried
            fore[which] = prior.astype(jnp.bfloat16).reshape(STEP, rows, cells)
            return inner

        lax.fori_loop(0, members // STEP, stencil, 0)

        for group in range(groups):
            lines = pl.ds(group * GROUP, GROUP)
            prior = fore[:, lines].reshape(wide, cells)

            def transform(part, inner, group=group, lines=lines, prior=prior):
                start = pl.multiple_of(part * 256, 256)
                result = jnp.dot(
                    block_diag[group, pl.ds(start, 256)],
                    prior,
                    preferred_element_type=jnp.float32,
                )
                many = 256 // GROUP
                done[field, pl.ds(part * many, many), lines] = result.astype(
                    jnp.bfloat16
                ).reshape(many, GROUP, cells)
                return inner

            lax.fori_loop(0, wide // 256, transform, 0)

        for step in range(1, n_mem):
            back(step, field).start()
        own_out(field).start()
        return carry

    lax.fori_loop(0, fields, work, 0)

    def finish_weight(step, carry):
        weight_to(step).wait_send()
        return carry

    lax.fori_loop(1, n_dom, finish_weight, 0)

    def finish(field, carry):
        for step in range(1, n_mem):
            forward(step, field).wait_send()

        @pl.when(here < n_dom - 1)
        def _():
            halo_up(field).wait_send()

        @pl.when(here > 0)
        def _():
            halo_down(field).wait_send()

        for step in range(1, n_mem):
            back(step, field).wait_send()
            back(step, field).wait_recv()
        own_out(field).wait()
        return carry

    lax.fori_loop(0, fields, finish, 0)


def per_device(state, wind_x, wind_y, viscosity_numbers, weights, obs_count, owner):
    n_mem = lax.axis_size("mem")
    n_dom = lax.axis_size("dom")
    local, fields, levels, rows, cells = state.shape
    members = local * n_mem
    groups = rows // GROUP
    wide = members * GROUP
    anywhere = pl.BlockSpec(memory_space=pl.ANY)
    scalars = pl.BlockSpec(memory_space=pltpu.SMEM)
    dma = pltpu.SemaphoreType.DMA
    return pl.pallas_call(
        functools.partial(kernel, n_mem, n_dom),
        out_shape=jax.ShapeDtypeStruct(state.shape, state.dtype),
        in_specs=[anywhere, anywhere, anywhere, scalars, anywhere, scalars, scalars],
        out_specs=anywhere,
        scratch_shapes=[
            pltpu.VMEM((fields, members, rows, cells), jnp.bfloat16),
            pltpu.VMEM((fields, members, GROUP, cells), jnp.bfloat16),
            pltpu.VMEM((fields, members, GROUP, cells), jnp.bfloat16),
            pltpu.VMEM((members, rows, cells), jnp.bfloat16),
            pltpu.VMEM((fields, members, rows, cells), jnp.bfloat16),
            pltpu.VMEM((groups, wide, wide), jnp.bfloat16),
            pltpu.VMEM((groups, wide, 128), jnp.float32),
            pltpu.VMEM((rows, members, members), jnp.float32),
            pltpu.VMEM((rows, members, members), jnp.bfloat16),
            pltpu.VMEM((rows, members, members), jnp.bfloat16),
            pltpu.VMEM((rows, cells), jnp.float32),
            pltpu.VMEM((rows, cells), jnp.float32),
            dma((n_mem - 1, fields)),
            dma((n_mem - 1, fields)),
            dma((fields,)),
            dma((2, fields)),
            dma((2, fields)),
            dma((n_mem - 1, fields)),
            dma((n_mem - 1, fields)),
            dma((fields,)),
            dma((n_dom,)),
            dma((n_dom,)),
            dma((4,)),
        ],
        compiler_params=pltpu.CompilerParams(
            collective_id=0, has_side_effects=True, vmem_limit_bytes=48 * 1024 * 1024
        ),
        cost_estimate=pl.CostEstimate(
            flops=4 * wide * wide * groups * fields * cells // 2,
            bytes_accessed=4 * state.size,
            transcendentals=0,
        ),
    )(state, wind_x, wind_y, viscosity_numbers, weights, obs_count, owner)


def solution(mesh):
    in_specs = (
        P("mem", None, None, "dom", None),
        P(None, "dom", None),
        P(None, "dom", None),
        P(),
        P("dom", None, None),
        P(),
        P(),
    )
    out_specs = P("mem", None, None, "dom", None)
    return jax.shard_map(
        per_device, mesh=mesh, in_specs=in_specs, out_specs=out_specs, check_vma=False
    )
```

```python
import functools

import jax
import jax.numpy as jnp
from jax import lax
from jax.experimental import pallas as pl
from jax.experimental.pallas import tpu as pltpu
from jax.sharding import PartitionSpec as P

OBS_HALF = 8
GROUP = 16
STEP = 4
MESH = pl.DeviceIdType.MESH


def partner(me, count, step):
    if count == 4:
        return (me + 1 - 2 * (me % 2), (me + 2) % 4, 3 - me)[step - 1]
    return (me + step) % count


def sender(me, count, step):
    return partner(me, count, step) if count == 4 else (me + count - step) % count


def kernel(
    n_mem,
    n_dom,
    state,
    wind_x,
    wind_y,
    viscosity_in,
    weights,
    obs_count_in,
    owner_in,
    out,
    raw,
    low,
    high,
    fore,
    done,
    block_diag,
    stacked,
    weight_in,
    weight_out,
    home,
    wx,
    wy,
    viscosity,
    obs_count,
    owner,
    sem_fwd_send,
    sem_fwd_recv,
    sem_own,
    sem_halo_send,
    sem_halo_recv,
    sem_ret_send,
    sem_ret_recv,
    sem_own_out,
    sem_w_send,
    sem_w_recv,
    sem_in,
):
    me = lax.axis_index("mem")
    here = lax.axis_index("dom")
    local, fields, _, rows, cells = state.shape
    members = local * n_mem
    per_owner = rows // n_dom
    groups = rows // GROUP

    weights_copy = pltpu.make_async_copy(weights, weight_in, sem_in.at[0])
    wx_copy = pltpu.make_async_copy(wind_x.at[me], wx, sem_in.at[1])
    wy_copy = pltpu.make_async_copy(wind_y.at[me], wy, sem_in.at[2])
    viscosity_copy = pltpu.make_async_copy(viscosity_in, viscosity, sem_in.at[4])
    count_copy = pltpu.make_async_copy(obs_count_in, obs_count, sem_in.at[5])
    owner_copy = pltpu.make_async_copy(owner_in, owner, sem_in.at[6])
    inputs = (weights_copy, wx_copy, wy_copy, viscosity_copy, count_copy, owner_copy)
    for copy in inputs:
        copy.start()

    barrier = pltpu.get_barrier_semaphore()
    for step in range(1, n_mem):
        pl.semaphore_signal(
            barrier, inc=1, device_id=(partner(me, n_mem, step), here), device_id_type=MESH
        )

    def greet(step, carry):
        pl.semaphore_signal(
            barrier, inc=1, device_id=(me, (here + step) % n_dom), device_id_type=MESH
        )
        return carry

    lax.fori_loop(1, n_dom, greet, 0)
    pl.semaphore_wait(barrier, n_mem - 1 + n_dom - 1)

    def forward(step, field):
        to = partner(me, n_mem, step)
        return pltpu.make_async_remote_copy(
            src_ref=state.at[:, field, to],
            dst_ref=raw.at[field, pl.ds(me * local, local)],
            send_sem=sem_fwd_send.at[step - 1, field],
            recv_sem=sem_fwd_recv.at[step - 1, field],
            device_id=(to, here),
            device_id_type=MESH,
        )

    def own(field):
        return pltpu.make_async_copy(
            state.at[:, field, me], raw.at[field, pl.ds(me * local, local)], sem_own.at[field]
        )

    def halo_up(field):
        return pltpu.make_async_remote_copy(
            src_ref=raw.at[field, :, pl.ds(rows - GROUP, GROUP)],
            dst_ref=low.at[field],
            send_sem=sem_halo_send.at[0, field],
            recv_sem=sem_halo_recv.at[0, field],
            device_id=(me, (here + 1) % n_dom),
            device_id_type=MESH,
        )

    def halo_down(field):
        return pltpu.make_async_remote_copy(
            src_ref=raw.at[field, :, pl.ds(0, GROUP)],
            dst_ref=high.at[field],
            send_sem=sem_halo_send.at[1, field],
            recv_sem=sem_halo_recv.at[1, field],
            device_id=(me, (here + n_dom - 1) % n_dom),
            device_id_type=MESH,
        )

    def back(step, field):
        to = partner(me, n_mem, step)
        return pltpu.make_async_remote_copy(
            src_ref=done.at[field, pl.ds(to * local, local)],
            dst_ref=out.at[:, field, me],
            send_sem=sem_ret_send.at[step - 1, field],
            recv_sem=sem_ret_recv.at[step - 1, field],
            device_id=(to, here),
            device_id_type=MESH,
        )

    def own_out(field):
        return pltpu.make_async_copy(
            done.at[field, pl.ds(me * local, local)], out.at[:, field, me], sem_own_out.at[field]
        )

    def weight_to(step):
        to = (here + step) % n_dom
        return pltpu.make_async_remote_copy(
            src_ref=weight_out.at[pl.ds(to * per_owner, per_owner)],
            dst_ref=home.at[pl.ds(here * per_owner, per_owner)],
            send_sem=sem_w_send.at[step],
            recv_sem=sem_w_recv.at[step],
            device_id=(me, to),
            device_id_type=MESH,
        )

    def send_field(field, carry):
        for step in range(1, n_mem):
            forward(step, field).start()
        own(field).start()
        return carry

    lax.fori_loop(0, fields, send_field, 0)

    weights_copy.wait()

    def narrow(block, carry):
        weight_out[block] = weight_in[block].astype(jnp.bfloat16)
        return carry

    lax.fori_loop(0, rows, narrow, 0)

    def send_weight(step, carry):
        weight_to(step).start()
        return carry

    lax.fori_loop(1, n_dom, send_weight, 0)
    own_weight = pltpu.make_async_copy(
        weight_out.at[pl.ds(here * per_owner, per_owner)],
        home.at[pl.ds(here * per_owner, per_owner)],
        sem_in.at[3],
    )
    own_weight.start()

    @pl.when(here == 0)
    def _():
        low[...] = jnp.zeros_like(low)

    @pl.when(here == n_dom - 1)
    def _():
        high[...] = jnp.zeros_like(high)

    def share_edges(field):
        own(field).wait()
        for step in range(1, n_mem):
            forward(step, field).wait_recv()

        @pl.when(here < n_dom - 1)
        def _():
            halo_up(field).start()

        @pl.when(here > 0)
        def _():
            halo_down(field).start()

    own_weight.wait()
    for copy in inputs[1:]:
        copy.wait()

    def take_weight(step, carry):
        weight_to(step).wait_recv()
        return carry

    lax.fori_loop(1, n_dom, take_weight, 0)

    row_id = lax.broadcasted_iota(jnp.int32, (members, members), 0)
    col_id = lax.broadcasted_iota(jnp.int32, (members, members), 1)
    eye = (row_id == col_id).astype(jnp.float32)
    eye_narrow = eye.astype(jnp.bfloat16)
    base = here * rows

    def combine(block, carry):
        mine = owner[base + block]

        def count(other, total):
            return total + jnp.where(owner[base + other] == mine, 1, 0)

        rank = lax.fori_loop(0, block, count, 0)
        weight = home[mine * per_owner + rank].astype(jnp.float32)
        number = jnp.full((members, members), obs_count[base + block], jnp.int32).astype(
            jnp.float32
        )
        gain = number / (number + OBS_HALF)
        mixing = (1.0 - gain) * eye + gain * weight
        square = (
            mixing - jnp.mean(mixing, axis=0, keepdims=True) + 1.0 / members
        ).astype(jnp.bfloat16)
        flipped = lax.dot_general(
            square, eye_narrow, (((0,), (0,)), ((), ())), preferred_element_type=jnp.float32
        )
        group = block // GROUP
        place = block % GROUP
        stacked[group, pl.ds(place, members, stride=GROUP), pl.ds(0, members)] = flipped
        return carry

    lax.fori_loop(0, rows, combine, 0)

    wide = members * GROUP
    spread_row = lax.broadcasted_iota(jnp.int32, (members, wide), 0)
    spread_col = lax.broadcasted_iota(jnp.int32, (members, wide), 1)
    spread = ((spread_col >> 4) == spread_row).astype(jnp.bfloat16)
    piece = 64
    mask = (
        (lax.broadcasted_iota(jnp.int32, (piece, wide), 0) & (GROUP - 1))
        == (lax.broadcasted_iota(jnp.int32, (piece, wide), 1) & (GROUP - 1))
    )

    for group in range(groups):

        def widen(part, carry, group=group):
            start = pl.multiple_of(part * piece, piece)
            lines = stacked[group, pl.ds(start, piece), pl.ds(0, members)].astype(jnp.bfloat16)
            full = jnp.dot(lines, spread, preferred_element_type=jnp.float32)
            block_diag[group, pl.ds(start, piece)] = jnp.where(mask, full, 0.0).astype(
                jnp.bfloat16
            )
            return carry

        lax.fori_loop(0, wide // piece, widen, 0)

    share_edges(0)

    flat = STEP * rows
    line = lax.broadcasted_iota(jnp.int32, (flat, cells), 0) & (rows - 1)
    cell = lax.broadcasted_iota(jnp.int32, (flat, cells), 1)
    first_line, last_line = line == 0, line == rows - 1
    first_cell, last_cell = cell == 0, cell == cells - 1
    blank = jnp.zeros((STEP, rows - GROUP, cells), jnp.float32)

    def work(field, carry):
        @pl.when(field < fields - 1)
        def _():
            share_edges(field + 1)

        @pl.when(here > 0)
        def _():
            halo_up(field).wait_recv()

        @pl.when(here < n_dom - 1)
        def _():
            halo_down(field).wait_recv()

        number = viscosity[field]
        along = jnp.broadcast_to(wx[...][None], (STEP, rows, cells)).reshape(flat, cells)
        across = jnp.broadcast_to(wy[...][None], (STEP, rows, cells)).reshape(flat, cells)

        def stencil(part, inner):
            which = pl.ds(part * STEP, STEP)
            middle = raw[field, which].astype(jnp.float32).reshape(flat, cells)
            under = low[field, which].astype(jnp.float32).reshape(STEP * GROUP, cells)
            over = high[field, which].astype(jnp.float32).reshape(STEP * GROUP, cells)
            under = pltpu.roll(under, STEP * GROUP - (GROUP - 1), 0).reshape(STEP, GROUP, cells)
            over = pltpu.roll(over, GROUP - 1, 0).reshape(STEP, GROUP, cells)
            under = jnp.concatenate([under, blank], axis=1).reshape(flat, cells)
            over = jnp.concatenate([blank, over], axis=1).reshape(flat, cells)
            lower = jnp.where(first_line, under, pltpu.roll(middle, 1, 0))
            upper = jnp.where(last_line, over, pltpu.roll(middle, flat - 1, 0))
            west = jnp.where(first_cell, 0.0, pltpu.roll(middle, 1, 1))
            east = jnp.where(last_cell, 0.0, pltpu.roll(middle, cells - 1, 1))
            ensemble = upper + lower + east + west - 4.0 * middle
            carried = along * (east - west) + across * (upper - lower)
            prior = middle + number * ensemble - 0.5 * carried
            fore[which] = prior.astype(jnp.bfloat16).reshape(STEP, rows, cells)
            return inner

        lax.fori_loop(0, members // STEP, stencil, 0)

        for group in range(groups):
            lines = pl.ds(group * GROUP, GROUP)
            prior = fore[:, lines].reshape(wide, cells)

            def transform(part, inner, group=group, lines=lines, prior=prior):
                start = pl.multiple_of(part * 256, 256)
                result = jnp.dot(
                    block_diag[group, pl.ds(start, 256)],
                    prior,
                    preferred_element_type=jnp.float32,
                )
                many = 256 // GROUP
                done[field, pl.ds(part * many, many), lines] = result.astype(
                    jnp.bfloat16
                ).reshape(many, GROUP, cells)
                return inner

            lax.fori_loop(0, wide // 256, transform, 0)

        for step in range(1, n_mem):
            back(step, field).start()
        own_out(field).start()
        return carry

    lax.fori_loop(0, fields, work, 0)

    def finish_weight(step, carry):
        weight_to(step).wait_send()
        return carry

    lax.fori_loop(1, n_dom, finish_weight, 0)

    def finish(field, carry):
        for step in range(1, n_mem):
            forward(step, field).wait_send()

        @pl.when(here < n_dom - 1)
        def _():
            halo_up(field).wait_send()

        @pl.when(here > 0)
        def _():
            halo_down(field).wait_send()

        for step in range(1, n_mem):
            back(step, field).wait_send()
            back(step, field).wait_recv()
        own_out(field).wait()
        return carry

    lax.fori_loop(0, fields, finish, 0)


def per_device(state, wind_x, wind_y, viscosity_numbers, weights, obs_count, owner):
    n_mem = lax.axis_size("mem")
    n_dom = lax.axis_size("dom")
    local, fields, levels, rows, cells = state.shape
    members = local * n_mem
    groups = rows // GROUP
    wide = members * GROUP
    anywhere = pl.BlockSpec(memory_space=pl.ANY)
    stay = pl.BlockSpec(memory_space=pltpu.HBM)
    dma = pltpu.SemaphoreType.DMA
    return pl.pallas_call(
        functools.partial(kernel, n_mem, n_dom),
        out_shape=jax.ShapeDtypeStruct(state.shape, state.dtype),
        in_specs=[stay] * 7,
        out_specs=anywhere,
        scratch_shapes=[
            pltpu.VMEM((fields, members, rows, cells), jnp.bfloat16),
            pltpu.VMEM((fields, members, GROUP, cells), jnp.bfloat16),
            pltpu.VMEM((fields, members, GROUP, cells), jnp.bfloat16),
            pltpu.VMEM((members, rows, cells), jnp.bfloat16),
            pltpu.VMEM((fields, members, rows, cells), jnp.bfloat16),
            pltpu.VMEM((groups, wide, wide), jnp.bfloat16),
            pltpu.VMEM((groups, wide, 128), jnp.float32),
            pltpu.VMEM((rows, members, members), jnp.float32),
            pltpu.VMEM((rows, members, members), jnp.bfloat16),
            pltpu.VMEM((rows, members, members), jnp.bfloat16),
            pltpu.VMEM((rows, cells), jnp.float32),
            pltpu.VMEM((rows, cells), jnp.float32),
            pltpu.SMEM(viscosity_numbers.shape, jnp.float32),
            pltpu.SMEM(obs_count.shape, jnp.int32),
            pltpu.SMEM(owner.shape, jnp.int32),
            dma((n_mem - 1, fields)),
            dma((n_mem - 1, fields)),
            dma((fields,)),
            dma((2, fields)),
            dma((2, fields)),
            dma((n_mem - 1, fields)),
            dma((n_mem - 1, fields)),
            dma((fields,)),
            dma((n_dom,)),
            dma((n_dom,)),
            dma((7,)),
        ],
        compiler_params=pltpu.CompilerParams(
            collective_id=0, has_side_effects=True, vmem_limit_bytes=48 * 1024 * 1024
        ),
        cost_estimate=pl.CostEstimate(
            flops=4 * wide * wide * groups * fields * cells // 2,
            bytes_accessed=4 * state.size,
            transcendentals=0,
        ),
    )(
        *(
            pltpu.with_memory_space_constraint(array, pltpu.HBM)
            for array in (state, wind_x, wind_y, viscosity_numbers, weights, obs_count, owner)
        )
    )


def solution(mesh):
    in_specs = (
        P("mem", None, None, "dom", None),
        P(None, "dom", None),
        P(None, "dom", None),
        P(),
        P("dom", None, None),
        P(),
        P(),
    )
    out_specs = P("mem", None, None, "dom", None)
    return jax.shard_map(
        per_device, mesh=mesh, in_specs=in_specs, out_specs=out_specs, check_vma=False
    )
```

```python
import functools

import jax
import jax.numpy as jnp
from jax import lax
from jax.experimental import pallas as pl
from jax.experimental.pallas import tpu as pltpu
from jax.sharding import PartitionSpec as P

OBS_HALF = 8
GROUP = 16
STEP = 4
MESH = pl.DeviceIdType.MESH


def partner(me, count, step):
    if count == 4:
        return (me + 1 - 2 * (me % 2), (me + 2) % 4, 3 - me)[step - 1]
    return (me + step) % count


def sender(me, count, step):
    return partner(me, count, step) if count == 4 else (me + count - step) % count


def kernel(
    n_mem,
    n_dom,
    state,
    wind_x,
    wind_y,
    viscosity_in,
    weights,
    obs_count_in,
    owner_in,
    out,
    raw,
    low,
    high,
    fore,
    done,
    block_diag,
    stacked,
    weight_in,
    weight_out,
    home,
    wx,
    wy,
    viscosity,
    obs_count,
    owner,
    sem_fwd_send,
    sem_fwd_recv,
    sem_own,
    sem_halo_send,
    sem_halo_recv,
    sem_ret_send,
    sem_ret_recv,
    sem_own_out,
    sem_w_send,
    sem_w_recv,
    sem_in,
    sem_met,
    sem_all,
):
    me = lax.axis_index("mem")
    here = lax.axis_index("dom")
    local, fields, _, rows, cells = state.shape
    members = local * n_mem
    per_owner = rows // n_dom
    groups = rows // GROUP

    weights_copy = pltpu.make_async_copy(weights, weight_in, sem_in.at[0])
    wx_copy = pltpu.make_async_copy(wind_x.at[me], wx, sem_in.at[1])
    wy_copy = pltpu.make_async_copy(wind_y.at[me], wy, sem_in.at[2])
    viscosity_copy = pltpu.make_async_copy(viscosity_in, viscosity, sem_in.at[4])
    count_copy = pltpu.make_async_copy(obs_count_in, obs_count, sem_in.at[5])
    owner_copy = pltpu.make_async_copy(owner_in, owner, sem_in.at[6])
    inputs = (weights_copy, wx_copy, wy_copy, viscosity_copy, count_copy, owner_copy)
    for copy in inputs:
        copy.start()

    barrier = pltpu.get_barrier_semaphore()
    gate = me == 0
    for step in range(1, n_mem):
        to = partner(me, n_mem, step)

        @pl.when(to != 0)
        def _(to=to):
            pl.semaphore_signal(barrier, inc=1, device_id=(to, here), device_id_type=MESH)

    @pl.when(jnp.logical_not(gate))
    def _():
        pl.semaphore_wait(barrier, n_mem - 1)
        pl.semaphore_signal(sem_met, inc=1, device_id=(0, here), device_id_type=MESH)

    @pl.when(gate)
    def _():
        pl.semaphore_wait(sem_met, n_mem - 1)

        def greet(step, carry):
            pl.semaphore_signal(
                barrier, inc=1, device_id=(0, (here + step) % n_dom), device_id_type=MESH
            )
            return carry

        lax.fori_loop(1, n_dom, greet, 0)

    def forward(step, field):
        to = partner(me, n_mem, step)
        return pltpu.make_async_remote_copy(
            src_ref=state.at[:, field, to],
            dst_ref=raw.at[field, pl.ds(me * local, local)],
            send_sem=sem_fwd_send.at[step - 1, field],
            recv_sem=sem_fwd_recv.at[step - 1, field],
            device_id=(to, here),
            device_id_type=MESH,
        )

    def own(field):
        return pltpu.make_async_copy(
            state.at[:, field, me], raw.at[field, pl.ds(me * local, local)], sem_own.at[field]
        )

    def halo_up(field):
        return pltpu.make_async_remote_copy(
            src_ref=raw.at[field, :, pl.ds(rows - GROUP, GROUP)],
            dst_ref=low.at[field],
            send_sem=sem_halo_send.at[0, field],
            recv_sem=sem_halo_recv.at[0, field],
            device_id=(me, (here + 1) % n_dom),
            device_id_type=MESH,
        )

    def halo_down(field):
        return pltpu.make_async_remote_copy(
            src_ref=raw.at[field, :, pl.ds(0, GROUP)],
            dst_ref=high.at[field],
            send_sem=sem_halo_send.at[1, field],
            recv_sem=sem_halo_recv.at[1, field],
            device_id=(me, (here + n_dom - 1) % n_dom),
            device_id_type=MESH,
        )

    def back(step, field):
        to = partner(me, n_mem, step)
        return pltpu.make_async_remote_copy(
            src_ref=done.at[field, pl.ds(to * local, local)],
            dst_ref=out.at[:, field, me],
            send_sem=sem_ret_send.at[step - 1, field],
            recv_sem=sem_ret_recv.at[step - 1, field],
            device_id=(to, here),
            device_id_type=MESH,
        )

    def own_out(field):
        return pltpu.make_async_copy(
            done.at[field, pl.ds(me * local, local)], out.at[:, field, me], sem_own_out.at[field]
        )

    def weight_to(step):
        to = (here + step) % n_dom
        return pltpu.make_async_remote_copy(
            src_ref=weight_out.at[pl.ds(to * per_owner, per_owner)],
            dst_ref=home.at[pl.ds(here * per_owner, per_owner)],
            send_sem=sem_w_send.at[step],
            recv_sem=sem_w_recv.at[step],
            device_id=(me, to),
            device_id_type=MESH,
        )

    def send_field(field, carry):
        for step in range(1, n_mem):
            forward(step, field).start()
        own(field).start()
        return carry

    lax.fori_loop(0, fields, send_field, 0)

    weights_copy.wait()

    def narrow(block, carry):
        weight_out[block] = weight_in[block].astype(jnp.bfloat16)
        return carry

    lax.fori_loop(0, rows, narrow, 0)

    @pl.when(gate)
    def _():
        pl.semaphore_wait(barrier, n_dom - 1)
        for other in range(1, n_mem):
            pl.semaphore_signal(sem_all, inc=1, device_id=(other, here), device_id_type=MESH)

    @pl.when(jnp.logical_not(gate))
    def _():
        pl.semaphore_wait(sem_all, 1)

    def send_weight(step, carry):
        weight_to(step).start()
        return carry

    lax.fori_loop(1, n_dom, send_weight, 0)
    own_weight = pltpu.make_async_copy(
        weight_out.at[pl.ds(here * per_owner, per_owner)],
        home.at[pl.ds(here * per_owner, per_owner)],
        sem_in.at[3],
    )
    own_weight.start()

    @pl.when(here == 0)
    def _():
        low[...] = jnp.zeros_like(low)

    @pl.when(here == n_dom - 1)
    def _():
        high[...] = jnp.zeros_like(high)

    def share_edges(field):
        own(field).wait()
        for step in range(1, n_mem):
            forward(step, field).wait_recv()

        @pl.when(here < n_dom - 1)
        def _():
            halo_up(field).start()

        @pl.when(here > 0)
        def _():
            halo_down(field).start()

    own_weight.wait()
    for copy in inputs[1:]:
        copy.wait()

    def take_weight(step, carry):
        weight_to(step).wait_recv()
        return carry

    lax.fori_loop(1, n_dom, take_weight, 0)

    row_id = lax.broadcasted_iota(jnp.int32, (members, members), 0)
    col_id = lax.broadcasted_iota(jnp.int32, (members, members), 1)
    eye = (row_id == col_id).astype(jnp.float32)
    eye_narrow = eye.astype(jnp.bfloat16)
    base = here * rows

    def combine(block, carry):
        mine = owner[base + block]

        def count(other, total):
            return total + jnp.where(owner[base + other] == mine, 1, 0)

        rank = lax.fori_loop(0, block, count, 0)
        weight = home[mine * per_owner + rank].astype(jnp.float32)
        number = jnp.full((members, members), obs_count[base + block], jnp.int32).astype(
            jnp.float32
        )
        gain = number / (number + OBS_HALF)
        mixing = (1.0 - gain) * eye + gain * weight
        square = (
            mixing - jnp.mean(mixing, axis=0, keepdims=True) + 1.0 / members
        ).astype(jnp.bfloat16)
        flipped = lax.dot_general(
            square, eye_narrow, (((0,), (0,)), ((), ())), preferred_element_type=jnp.float32
        )
        group = block // GROUP
        place = block % GROUP
        stacked[group, pl.ds(place, members, stride=GROUP), pl.ds(0, members)] = flipped
        return carry

    lax.fori_loop(0, rows, combine, 0)

    wide = members * GROUP
    spread_row = lax.broadcasted_iota(jnp.int32, (members, wide), 0)
    spread_col = lax.broadcasted_iota(jnp.int32, (members, wide), 1)
    spread = ((spread_col >> 4) == spread_row).astype(jnp.bfloat16)
    piece = 64
    mask = (
        (lax.broadcasted_iota(jnp.int32, (piece, wide), 0) & (GROUP - 1))
        == (lax.broadcasted_iota(jnp.int32, (piece, wide), 1) & (GROUP - 1))
    )

    for group in range(groups):

        def widen(part, carry, group=group):
            start = pl.multiple_of(part * piece, piece)
            lines = stacked[group, pl.ds(start, piece), pl.ds(0, members)].astype(jnp.bfloat16)
            full = jnp.dot(lines, spread, preferred_element_type=jnp.float32)
            block_diag[group, pl.ds(start, piece)] = jnp.where(mask, full, 0.0).astype(
                jnp.bfloat16
            )
            return carry

        lax.fori_loop(0, wide // piece, widen, 0)

    share_edges(0)

    flat = STEP * rows
    line = lax.broadcasted_iota(jnp.int32, (flat, cells), 0) & (rows - 1)
    cell = lax.broadcasted_iota(jnp.int32, (flat, cells), 1)
    first_line, last_line = line == 0, line == rows - 1
    first_cell, last_cell = cell == 0, cell == cells - 1
    blank = jnp.zeros((STEP, rows - GROUP, cells), jnp.float32)

    def work(field, carry):
        @pl.when(field < fields - 1)
        def _():
            share_edges(field + 1)

        @pl.when(here > 0)
        def _():
            halo_up(field).wait_recv()

        @pl.when(here < n_dom - 1)
        def _():
            halo_down(field).wait_recv()

        number = viscosity[field]
        along = jnp.broadcast_to(wx[...][None], (STEP, rows, cells)).reshape(flat, cells)
        across = jnp.broadcast_to(wy[...][None], (STEP, rows, cells)).reshape(flat, cells)

        def stencil(part, inner):
            which = pl.ds(part * STEP, STEP)
            middle = raw[field, which].astype(jnp.float32).reshape(flat, cells)
            under = low[field, which].astype(jnp.float32).reshape(STEP * GROUP, cells)
            over = high[field, which].astype(jnp.float32).reshape(STEP * GROUP, cells)
            under = pltpu.roll(under, STEP * GROUP - (GROUP - 1), 0).reshape(STEP, GROUP, cells)
            over = pltpu.roll(over, GROUP - 1, 0).reshape(STEP, GROUP, cells)
            under = jnp.concatenate([under, blank], axis=1).reshape(flat, cells)
            over = jnp.concatenate([blank, over], axis=1).reshape(flat, cells)
            lower = jnp.where(first_line, under, pltpu.roll(middle, 1, 0))
            upper = jnp.where(last_line, over, pltpu.roll(middle, flat - 1, 0))
            west = jnp.where(first_cell, 0.0, pltpu.roll(middle, 1, 1))
            east = jnp.where(last_cell, 0.0, pltpu.roll(middle, cells - 1, 1))
            ensemble = upper + lower + east + west - 4.0 * middle
            carried = along * (east - west) + across * (upper - lower)
            prior = middle + number * ensemble - 0.5 * carried
            fore[which] = prior.astype(jnp.bfloat16).reshape(STEP, rows, cells)
            return inner

        lax.fori_loop(0, members // STEP, stencil, 0)

        for group in range(groups):
            lines = pl.ds(group * GROUP, GROUP)
            prior = fore[:, lines].reshape(wide, cells)

            def transform(part, inner, group=group, lines=lines, prior=prior):
                start = pl.multiple_of(part * 256, 256)
                result = jnp.dot(
                    block_diag[group, pl.ds(start, 256)],
                    prior,
                    preferred_element_type=jnp.float32,
                )
                many = 256 // GROUP
                done[field, pl.ds(part * many, many), lines] = result.astype(
                    jnp.bfloat16
                ).reshape(many, GROUP, cells)
                return inner

            lax.fori_loop(0, wide // 256, transform, 0)

        for step in range(1, n_mem):
            back(step, field).start()
        own_out(field).start()
        return carry

    lax.fori_loop(0, fields, work, 0)

    def finish_weight(step, carry):
        weight_to(step).wait_send()
        return carry

    lax.fori_loop(1, n_dom, finish_weight, 0)

    def finish(field, carry):
        for step in range(1, n_mem):
            forward(step, field).wait_send()

        @pl.when(here < n_dom - 1)
        def _():
            halo_up(field).wait_send()

        @pl.when(here > 0)
        def _():
            halo_down(field).wait_send()

        for step in range(1, n_mem):
            back(step, field).wait_send()
            back(step, field).wait_recv()
        own_out(field).wait()
        return carry

    lax.fori_loop(0, fields, finish, 0)


def per_device(state, wind_x, wind_y, viscosity_numbers, weights, obs_count, owner):
    n_mem = lax.axis_size("mem")
    n_dom = lax.axis_size("dom")
    local, fields, levels, rows, cells = state.shape
    members = local * n_mem
    groups = rows // GROUP
    wide = members * GROUP
    anywhere = pl.BlockSpec(memory_space=pl.ANY)
    stay = pl.BlockSpec(memory_space=pltpu.HBM)
    dma = pltpu.SemaphoreType.DMA
    return pl.pallas_call(
        functools.partial(kernel, n_mem, n_dom),
        out_shape=jax.ShapeDtypeStruct(state.shape, state.dtype),
        in_specs=[stay] * 7,
        out_specs=anywhere,
        scratch_shapes=[
            pltpu.VMEM((fields, members, rows, cells), jnp.bfloat16),
            pltpu.VMEM((fields, members, GROUP, cells), jnp.bfloat16),
            pltpu.VMEM((fields, members, GROUP, cells), jnp.bfloat16),
            pltpu.VMEM((members, rows, cells), jnp.bfloat16),
            pltpu.VMEM((fields, members, rows, cells), jnp.bfloat16),
            pltpu.VMEM((groups, wide, wide), jnp.bfloat16),
            pltpu.VMEM((groups, wide, 128), jnp.float32),
            pltpu.VMEM((rows, members, members), jnp.float32),
            pltpu.VMEM((rows, members, members), jnp.bfloat16),
            pltpu.VMEM((rows, members, members), jnp.bfloat16),
            pltpu.VMEM((rows, cells), jnp.float32),
            pltpu.VMEM((rows, cells), jnp.float32),
            pltpu.SMEM(viscosity_numbers.shape, jnp.float32),
            pltpu.SMEM(obs_count.shape, jnp.int32),
            pltpu.SMEM(owner.shape, jnp.int32),
            dma((n_mem - 1, fields)),
            dma((n_mem - 1, fields)),
            dma((fields,)),
            dma((2, fields)),
            dma((2, fields)),
            dma((n_mem - 1, fields)),
            dma((n_mem - 1, fields)),
            dma((fields,)),
            dma((n_dom,)),
            dma((n_dom,)),
            dma((7,)),
            pltpu.SemaphoreType.REGULAR,
            pltpu.SemaphoreType.REGULAR,
        ],
        compiler_params=pltpu.CompilerParams(
            collective_id=0, has_side_effects=True, vmem_limit_bytes=48 * 1024 * 1024
        ),
        cost_estimate=pl.CostEstimate(
            flops=4 * wide * wide * groups * fields * cells // 2,
            bytes_accessed=4 * state.size,
            transcendentals=0,
        ),
    )(
        *(
            pltpu.with_memory_space_constraint(array, pltpu.HBM)
            for array in (state, wind_x, wind_y, viscosity_numbers, weights, obs_count, owner)
        )
    )


def solution(mesh):
    in_specs = (
        P("mem", None, None, "dom", None),
        P(None, "dom", None),
        P(None, "dom", None),
        P(),
        P("dom", None, None),
        P(),
        P(),
    )
    out_specs = P("mem", None, None, "dom", None)
    return jax.shard_map(
        per_device, mesh=mesh, in_specs=in_specs, out_specs=out_specs, check_vma=False
    )
```

```python
import functools

import jax
import jax.numpy as jnp
from jax import lax
from jax.experimental import pallas as pl
from jax.experimental.pallas import tpu as pltpu
from jax.sharding import PartitionSpec as P

OBS_HALF = 8
GROUP = 16
STEP = 4
MESH = pl.DeviceIdType.MESH


def partner(me, count, step):
    if count == 4:
        return (me + 1 - 2 * (me % 2), (me + 2) % 4, 3 - me)[step - 1]
    return (me + step) % count


def sender(me, count, step):
    return partner(me, count, step) if count == 4 else (me + count - step) % count


def kernel(
    n_mem,
    n_dom,
    state,
    wind_x,
    wind_y,
    viscosity_in,
    weights,
    obs_count_in,
    owner_in,
    out,
    raw,
    low,
    high,
    fore,
    done,
    block_diag,
    stacked,
    weight_in,
    weight_out,
    home,
    wx,
    wy,
    viscosity,
    obs_count,
    owner,
    place_of,
    sem_fwd_send,
    sem_fwd_recv,
    sem_own,
    sem_halo_send,
    sem_halo_recv,
    sem_ret_send,
    sem_ret_recv,
    sem_own_out,
    sem_w_send,
    sem_w_recv,
    sem_in,
    sem_met,
    sem_all,
):
    me = lax.axis_index("mem")
    here = lax.axis_index("dom")
    local, fields, _, rows, cells = state.shape
    members = local * n_mem
    per_owner = rows // n_dom
    groups = rows // GROUP

    weights_copy = pltpu.make_async_copy(weights, weight_in, sem_in.at[0])
    wx_copy = pltpu.make_async_copy(wind_x.at[me], wx, sem_in.at[1])
    wy_copy = pltpu.make_async_copy(wind_y.at[me], wy, sem_in.at[2])
    viscosity_copy = pltpu.make_async_copy(viscosity_in, viscosity, sem_in.at[4])
    count_copy = pltpu.make_async_copy(obs_count_in, obs_count, sem_in.at[5])
    owner_copy = pltpu.make_async_copy(owner_in, owner, sem_in.at[6])
    inputs = (weights_copy, wx_copy, wy_copy, viscosity_copy, count_copy, owner_copy)
    for copy in inputs:
        copy.start()

    barrier = pltpu.get_barrier_semaphore()
    gate = me == 0
    for step in range(1, n_mem):
        to = partner(me, n_mem, step)

        @pl.when(to != 0)
        def _(to=to):
            pl.semaphore_signal(barrier, inc=1, device_id=(to, here), device_id_type=MESH)

    @pl.when(jnp.logical_not(gate))
    def _():
        pl.semaphore_wait(barrier, n_mem - 1)
        pl.semaphore_signal(sem_met, inc=1, device_id=(0, here), device_id_type=MESH)

    @pl.when(gate)
    def _():
        pl.semaphore_wait(sem_met, n_mem - 1)

        def greet(step, carry):
            pl.semaphore_signal(
                barrier, inc=1, device_id=(0, (here + step) % n_dom), device_id_type=MESH
            )
            return carry

        lax.fori_loop(1, n_dom, greet, 0)


    def forward(step, field):
        to = partner(me, n_mem, step)
        return pltpu.make_async_remote_copy(
            src_ref=state.at[:, field, to],
            dst_ref=raw.at[field, pl.ds(me * local, local)],
            send_sem=sem_fwd_send.at[step - 1, field],
            recv_sem=sem_fwd_recv.at[step - 1, field],
            device_id=(to, here),
            device_id_type=MESH,
        )

    def own(field):
        return pltpu.make_async_copy(
            state.at[:, field, me], raw.at[field, pl.ds(me * local, local)], sem_own.at[field]
        )

    def halo_up(field):
        return pltpu.make_async_remote_copy(
            src_ref=raw.at[field, :, pl.ds(rows - GROUP, GROUP)],
            dst_ref=low.at[field],
            send_sem=sem_halo_send.at[0, field],
            recv_sem=sem_halo_recv.at[0, field],
            device_id=(me, (here + 1) % n_dom),
            device_id_type=MESH,
        )

    def halo_down(field):
        return pltpu.make_async_remote_copy(
            src_ref=raw.at[field, :, pl.ds(0, GROUP)],
            dst_ref=high.at[field],
            send_sem=sem_halo_send.at[1, field],
            recv_sem=sem_halo_recv.at[1, field],
            device_id=(me, (here + n_dom - 1) % n_dom),
            device_id_type=MESH,
        )

    def back(step, field):
        to = partner(me, n_mem, step)
        return pltpu.make_async_remote_copy(
            src_ref=done.at[field, pl.ds(to * local, local)],
            dst_ref=out.at[:, field, me],
            send_sem=sem_ret_send.at[step - 1, field],
            recv_sem=sem_ret_recv.at[step - 1, field],
            device_id=(to, here),
            device_id_type=MESH,
        )

    def own_out(field):
        return pltpu.make_async_copy(
            done.at[field, pl.ds(me * local, local)], out.at[:, field, me], sem_own_out.at[field]
        )

    def weight_to(step):
        to = (here + step) % n_dom
        return pltpu.make_async_remote_copy(
            src_ref=weight_out.at[pl.ds(to * per_owner, per_owner)],
            dst_ref=home.at[pl.ds(here * per_owner, per_owner)],
            send_sem=sem_w_send.at[step],
            recv_sem=sem_w_recv.at[step],
            device_id=(me, to),
            device_id_type=MESH,
        )

    def send_field(field, carry):
        for step in range(1, n_mem):
            forward(step, field).start()
        own(field).start()
        return carry

    lax.fori_loop(0, fields, send_field, 0)

    weights_copy.wait()

    def narrow(block, carry):
        weight_out[block] = weight_in[block].astype(jnp.bfloat16)
        return carry

    lax.fori_loop(0, rows, narrow, 0)

    @pl.when(gate)
    def _():
        pl.semaphore_wait(barrier, n_dom - 1)
        for other in range(1, n_mem):
            pl.semaphore_signal(sem_all, inc=1, device_id=(other, here), device_id_type=MESH)

    @pl.when(jnp.logical_not(gate))
    def _():
        pl.semaphore_wait(sem_all, 1)

    def send_weight(step, carry):
        weight_to(step).start()
        return carry

    lax.fori_loop(1, n_dom, send_weight, 0)
    own_weight = pltpu.make_async_copy(
        weight_out.at[pl.ds(here * per_owner, per_owner)],
        home.at[pl.ds(here * per_owner, per_owner)],
        sem_in.at[3],
    )
    own_weight.start()


    @pl.when(here == 0)
    def _():
        low[...] = jnp.zeros_like(low)

    @pl.when(here == n_dom - 1)
    def _():
        high[...] = jnp.zeros_like(high)

    def share_edges(field):
        own(field).wait()
        for step in range(1, n_mem):
            forward(step, field).wait_recv()

        @pl.when(here < n_dom - 1)
        def _():
            halo_up(field).start()

        @pl.when(here > 0)
        def _():
            halo_down(field).start()

    for copy in inputs[1:]:
        copy.wait()
    base = here * rows

    def locate(block, carry):
        mine = owner[base + block]

        def count(other, total):
            return total + jnp.where(owner[base + other] == mine, 1, 0)

        place_of[block] = mine * per_owner + lax.fori_loop(0, block, count, 0)
        return carry

    lax.fori_loop(0, rows, locate, 0)
    share_edges(0)
    own_weight.wait()

    def take_weight(step, carry):
        weight_to(step).wait_recv()
        return carry

    lax.fori_loop(1, n_dom, take_weight, 0)

    row_id = lax.broadcasted_iota(jnp.int32, (members, members), 0)
    col_id = lax.broadcasted_iota(jnp.int32, (members, members), 1)
    eye = (row_id == col_id).astype(jnp.float32)
    eye_narrow = eye.astype(jnp.bfloat16)

    def combine(block, carry):
        weight = home[place_of[block]].astype(jnp.float32)
        number = jnp.full((members, members), obs_count[base + block], jnp.int32).astype(
            jnp.float32
        )
        gain = number / (number + OBS_HALF)
        mixing = (1.0 - gain) * eye + gain * weight
        square = (
            mixing - jnp.mean(mixing, axis=0, keepdims=True) + 1.0 / members
        ).astype(jnp.bfloat16)
        flipped = lax.dot_general(
            square, eye_narrow, (((0,), (0,)), ((), ())), preferred_element_type=jnp.float32
        )
        group = block // GROUP
        place = block % GROUP
        stacked[group, pl.ds(place, members, stride=GROUP), pl.ds(0, members)] = flipped
        return carry

    lax.fori_loop(0, rows, combine, 0, unroll=4)
    share_edges(1)

    wide = members * GROUP
    spread_row = lax.broadcasted_iota(jnp.int32, (members, wide), 0)
    spread_col = lax.broadcasted_iota(jnp.int32, (members, wide), 1)
    spread = ((spread_col >> 4) == spread_row).astype(jnp.bfloat16)
    piece = 64
    mask = (
        (lax.broadcasted_iota(jnp.int32, (piece, wide), 0) & (GROUP - 1))
        == (lax.broadcasted_iota(jnp.int32, (piece, wide), 1) & (GROUP - 1))
    )

    for group in range(groups):

        def widen(part, carry, group=group):
            start = pl.multiple_of(part * piece, piece)
            lines = stacked[group, pl.ds(start, piece), pl.ds(0, members)].astype(jnp.bfloat16)
            full = jnp.dot(lines, spread, preferred_element_type=jnp.float32)
            block_diag[group, pl.ds(start, piece)] = jnp.where(mask, full, 0.0).astype(
                jnp.bfloat16
            )
            return carry

        lax.fori_loop(0, wide // piece, widen, 0)


    flat = STEP * rows
    line = lax.broadcasted_iota(jnp.int32, (flat, cells), 0) & (rows - 1)
    cell = lax.broadcasted_iota(jnp.int32, (flat, cells), 1)
    first_line, last_line = line == 0, line == rows - 1
    first_cell, last_cell = cell == 0, cell == cells - 1
    blank = jnp.zeros((STEP, rows - GROUP, cells), jnp.float32)

    def work(field, carry):
        @pl.when(here > 0)
        def _():
            halo_up(field).wait_recv()

        @pl.when(here < n_dom - 1)
        def _():
            halo_down(field).wait_recv()

        number = viscosity[field]
        along = jnp.broadcast_to(wx[...][None], (STEP, rows, cells)).reshape(flat, cells)
        across = jnp.broadcast_to(wy[...][None], (STEP, rows, cells)).reshape(flat, cells)

        def stencil(part, inner):
            which = pl.ds(part * STEP, STEP)
            middle = raw[field, which].astype(jnp.float32).reshape(flat, cells)
            under = low[field, which].astype(jnp.float32).reshape(STEP * GROUP, cells)
            over = high[field, which].astype(jnp.float32).reshape(STEP * GROUP, cells)
            under = pltpu.roll(under, STEP * GROUP - (GROUP - 1), 0).reshape(STEP, GROUP, cells)
            over = pltpu.roll(over, GROUP - 1, 0).reshape(STEP, GROUP, cells)
            under = jnp.concatenate([under, blank], axis=1).reshape(flat, cells)
            over = jnp.concatenate([blank, over], axis=1).reshape(flat, cells)
            lower = jnp.where(first_line, under, pltpu.roll(middle, 1, 0))
            upper = jnp.where(last_line, over, pltpu.roll(middle, flat - 1, 0))
            west = jnp.where(first_cell, 0.0, pltpu.roll(middle, 1, 1))
            east = jnp.where(last_cell, 0.0, pltpu.roll(middle, cells - 1, 1))
            ensemble = upper + lower + east + west - 4.0 * middle
            carried = along * (east - west) + across * (upper - lower)
            prior = middle + number * ensemble - 0.5 * carried
            fore[which] = prior.astype(jnp.bfloat16).reshape(STEP, rows, cells)
            return inner

        lax.fori_loop(0, members // STEP, stencil, 0)

        for group in range(groups):
            lines = pl.ds(group * GROUP, GROUP)
            prior = fore[:, lines].reshape(wide, cells)

            def transform(part, inner, group=group, lines=lines, prior=prior):
                start = pl.multiple_of(part * 256, 256)
                result = jnp.dot(
                    block_diag[group, pl.ds(start, 256)],
                    prior,
                    preferred_element_type=jnp.float32,
                )
                many = 256 // GROUP
                done[field, pl.ds(part * many, many), lines] = result.astype(
                    jnp.bfloat16
                ).reshape(many, GROUP, cells)
                return inner

            lax.fori_loop(0, wide // 256, transform, 0)

        for step in range(1, n_mem):
            back(step, field).start()
        own_out(field).start()

        @pl.when(field < fields - 2)
        def _():
            share_edges(field + 2)

        return carry

    lax.fori_loop(0, fields, work, 0)

    def finish_weight(step, carry):
        weight_to(step).wait_send()
        return carry

    lax.fori_loop(1, n_dom, finish_weight, 0)

    def finish(field, carry):
        for step in range(1, n_mem):
            forward(step, field).wait_send()

        @pl.when(here < n_dom - 1)
        def _():
            halo_up(field).wait_send()

        @pl.when(here > 0)
        def _():
            halo_down(field).wait_send()

        for step in range(1, n_mem):
            back(step, field).wait_send()
            back(step, field).wait_recv()
        own_out(field).wait()
        return carry

    lax.fori_loop(0, fields, finish, 0)


def per_device(state, wind_x, wind_y, viscosity_numbers, weights, obs_count, owner):
    n_mem = lax.axis_size("mem")
    n_dom = lax.axis_size("dom")
    local, fields, levels, rows, cells = state.shape
    members = local * n_mem
    groups = rows // GROUP
    wide = members * GROUP
    anywhere = pl.BlockSpec(memory_space=pl.ANY)
    stay = pl.BlockSpec(memory_space=pltpu.HBM)
    dma = pltpu.SemaphoreType.DMA
    return pl.pallas_call(
        functools.partial(kernel, n_mem, n_dom),
        out_shape=jax.ShapeDtypeStruct(state.shape, state.dtype),
        in_specs=[stay] * 7,
        out_specs=anywhere,
        scratch_shapes=[
            pltpu.VMEM((fields, members, rows, cells), jnp.bfloat16),
            pltpu.VMEM((fields, members, GROUP, cells), jnp.bfloat16),
            pltpu.VMEM((fields, members, GROUP, cells), jnp.bfloat16),
            pltpu.VMEM((members, rows, cells), jnp.bfloat16),
            pltpu.VMEM((fields, members, rows, cells), jnp.bfloat16),
            pltpu.VMEM((groups, wide, wide), jnp.bfloat16),
            pltpu.VMEM((groups, wide, 128), jnp.float32),
            pltpu.VMEM((rows, members, members), jnp.float32),
            pltpu.VMEM((rows, members, members), jnp.bfloat16),
            pltpu.VMEM((rows, members, members), jnp.bfloat16),
            pltpu.VMEM((rows, cells), jnp.float32),
            pltpu.VMEM((rows, cells), jnp.float32),
            pltpu.SMEM(viscosity_numbers.shape, jnp.float32),
            pltpu.SMEM(obs_count.shape, jnp.int32),
            pltpu.SMEM(owner.shape, jnp.int32),
            pltpu.SMEM((rows,), jnp.int32),
            dma((n_mem - 1, fields)),
            dma((n_mem - 1, fields)),
            dma((fields,)),
            dma((2, fields)),
            dma((2, fields)),
            dma((n_mem - 1, fields)),
            dma((n_mem - 1, fields)),
            dma((fields,)),
            dma((n_dom,)),
            dma((n_dom,)),
            dma((7,)),
            pltpu.SemaphoreType.REGULAR,
            pltpu.SemaphoreType.REGULAR,
        ],
        compiler_params=pltpu.CompilerParams(
            collective_id=0, has_side_effects=True, vmem_limit_bytes=48 * 1024 * 1024
        ),
        cost_estimate=pl.CostEstimate(
            flops=4 * wide * wide * groups * fields * cells // 2,
            bytes_accessed=4 * state.size,
            transcendentals=0,
        ),
    )(
        *(
            pltpu.with_memory_space_constraint(array, pltpu.HBM)
            for array in (state, wind_x, wind_y, viscosity_numbers, weights, obs_count, owner)
        )
    )


def solution(mesh):
    in_specs = (
        P("mem", None, None, "dom", None),
        P(None, "dom", None),
        P(None, "dom", None),
        P(),
        P("dom", None, None),
        P(),
        P(),
    )
    out_specs = P("mem", None, None, "dom", None)
    return jax.shard_map(
        per_device, mesh=mesh, in_specs=in_specs, out_specs=out_specs, check_vma=False
    )
```
